32 devices in a mesh: dp: 2 (over y), expert: 16 (over z, x, core).
Axes of the slice: x: 2, y: 2, z: 4, core: 2. Of those that a mesh axis runs over, the one named last changes fastest.
Arguments:
- tokens: bfloat16 [4096, 1920], P(('dp', 'expert')), may hold values from -10 to 10
- assignment: int32 [4096], P(('dp', 'expert')), may hold values from 0 to 15, as said below
- centroids: bfloat16 [16, 1920], P('expert'), may hold values from -0.125 to 0.125
- norm_gain: float32 [16, 1920], P('expert'), may hold values from 0.25 to 1.75
- inner_weight: bfloat16 [16, 4096, 1920], P('expert', 'dp'), may hold values from -0.125 to 0.125
- outer_weight: bfloat16 [16, 4096, 1920], P('expert', 'dp'), may hold values from -0.09375 to 0.09375
Outputs:
- layer_out: bfloat16 [4096, 1920], P(('dp', 'expert'))
The draws below stay inside these ranges and needn't reach their ends.
Inputs may be any that keep to these rules, and one draw needn't show every extreme that they name: `assignment`: each expert is assigned exactly 128 of the tokens of the devices that share one index of dp. One device assigns at most 16 of its tokens to one expert, and every expert gets exactly 16 tokens from some device of each index of dp.
All inputs are finite; a program needn't handle non-finite values.
Results may differ from the reference program's by a relative error of at most 0.007.
Values may be sent and summed in bfloat16 or wider, within the bound.
No kernel may reach another device: no remote copies, remote signals or barrier semaphores. Data moves between devices by JAX's collectives and lax.ppermute only.
A program may use at most 64 MiB of HBM per device.

```python
import jax
import jax.numpy as jnp
from jax import lax

D = 1920
FF = 4096
TOK_DEV = 128
EXPERTS = 16
CAP = 16
TOKENS = 4096
N_DP = 2
N_EXPERT = 16


def draw_tokens(key, part):
    normal_key = jax.random.fold_in(key, 0)
    values = jax.random.normal(normal_key, (TOKENS, D), jnp.float32)
    return jnp.clip(values, -10.0, 10.0).astype(jnp.bfloat16)


def draw_assignment(key, part):

    def one_row(row_key):
        pool_key, source_key, expert_key, order_key = jax.random.split(row_key, 4)
        pool = jnp.repeat(jnp.arange(1, EXPERTS, dtype=jnp.int32), CAP)
        picked = jax.random.permutation(pool_key, pool)[:TOK_DEV - CAP]
        offsets_row = jnp.concatenate([jnp.zeros((CAP,), jnp.int32), picked])
        shift_perm = jax.random.permutation(source_key, N_EXPERT).astype(jnp.int32)
        relabel = jax.random.permutation(expert_key, EXPERTS).astype(jnp.int32)

        def one_source(source_index):
            token_order = jax.random.permutation(jax.random.fold_in(order_key, source_index), TOK_DEV)
            return relabel[(shift_perm[source_index] + offsets_row[token_order]) % EXPERTS]
        return jax.vmap(one_source)(jnp.arange(N_EXPERT, dtype=jnp.int32))
    row_keys = jax.vmap(lambda index: jax.random.fold_in(key, index))(jnp.arange(N_DP, dtype=jnp.int32))
    table = jax.vmap(one_row)(row_keys)
    return table.reshape(-1).astype(jnp.int32)


def level_of(own_key, extent, shards, least, largest):
    def one(position, parts):
        heights = jax.random.uniform(jax.random.fold_in(jax.random.fold_in(own_key, 6), position), (parts,), jnp.float32, least / len(shards), largest / len(shards))
        return jnp.repeat(jnp.exp(heights), extent[position] // parts).reshape((-1,) + (1,) * (len(extent) - position - 1))

    gain = one(*shards[0])
    for cut in shards[1:]:
        gain = gain * one(*cut)
    return gain


def normal_values(stream_key, dims, deviation, limit, cuts=(), kind=jnp.bfloat16):
    loudness = level_of(stream_key, dims, cuts, -0.22, 0.18) if cuts else 1.0
    result = jax.random.normal(stream_key, dims, jnp.float32) * deviation * loudness
    return jnp.minimum(jnp.maximum(result, -limit), limit).astype(kind)


def setup_inputs(seed: int = 0) -> dict:
    arg_keys = jax.random.split(jax.random.key(seed), 7)
    tokens = draw_tokens(jax.random.fold_in(arg_keys[6], 71), 0)
    assignment = draw_assignment(jax.random.fold_in(arg_keys[6], 71), 0)
    centroids = normal_values(arg_keys[2], (EXPERTS, D), D ** -0.5, 0.125, ((0, 16),))
    norm_gain = jnp.clip(1.0 + 0.15 * jax.random.normal(arg_keys[3], (EXPERTS, D), jnp.float32), 0.25, 1.75)
    inner_weight = normal_values(arg_keys[4], (EXPERTS, FF, D), D ** -0.5, 0.125, ((0, 16), (1, 2)))
    outer_weight = normal_values(arg_keys[5], (EXPERTS, FF, D), FF ** -0.5, 0.09375, ((0, 16), (1, 2)))
    return dict(tokens=tokens, assignment=assignment, centroids=centroids, norm_gain=norm_gain, inner_weight=inner_weight, outer_weight=outer_weight)


epsilon = 1e-05

def normalize(rows_in, gain_row):
    values = rows_in.astype(jnp.float32)
    center = lax.optimization_barrier(jnp.mean(values, axis=1, keepdims=True))
    spread = lax.optimization_barrier(jnp.mean(jnp.square(values - center), axis=1, keepdims=True))
    return ((values - center) * lax.rsqrt(spread + epsilon) * gain_row).astype(jnp.bfloat16)

def reference(tokens, assignment, centroids, norm_gain, inner_weight, outer_weight):
    per_expert = TOK_DEV * N_DP
    share = FF // N_DP
    order = jnp.argsort(assignment, stable=True).astype(jnp.int32)
    grouped = order.reshape(EXPERTS, per_expert)

    def one_expert(operands):
        index_rows, gain_row, inner_mat, outer_mat = operands
        normed = normalize(jnp.take(tokens, index_rows, axis=0), gain_row[None, :])
        inner_act = lax.dot_general(normed, inner_mat, (((1,), (1,)), ((), ())), preferred_element_type=jnp.float32)
        hidden = jnp.maximum(inner_act, 0.0).astype(jnp.bfloat16)
        total = jnp.zeros((per_expert, D), jnp.float32)
        for group in range(N_DP):
            part_sum = jnp.dot(hidden[:, group * share:(group + 1) * share], outer_mat[group * share:(group + 1) * share], preferred_element_type=jnp.float32)
            rounded = lax.optimization_barrier(part_sum.astype(jnp.bfloat16))
            total = total + rounded.astype(jnp.float32)
        return total.astype(jnp.bfloat16)
    outputs = lax.map(one_expert, (grouped, norm_gain, inner_weight, outer_weight))
    expert_out = jnp.zeros((EXPERTS * per_expert, D), jnp.bfloat16).at[grouped.reshape(-1)].set(outputs.reshape(-1, D))
    scores = jnp.dot(tokens, centroids.T, preferred_element_type=jnp.float32)
    chosen = jnp.take_along_axis(scores, assignment[:, None], axis=1)[:, 0]
    gate_value = jax.nn.sigmoid(chosen).astype(jnp.bfloat16)
    mixed_out = tokens.astype(jnp.float32) + gate_value.astype(jnp.float32)[:, None] * expert_out.astype(jnp.float32)
    return mixed_out.astype(jnp.bfloat16)
```

```python
import functools

import jax
import jax.numpy as jnp
from jax import lax
from jax.experimental import pallas as pl
from jax.experimental.pallas import tpu as pltpu
from jax.sharding import PartitionSpec as P

EPSILON = 1e-05
EMPTY = 64.0
VMEM_LIMIT = 48 * 1024 * 1024


def whole(shape):
    return pl.BlockSpec(shape, lambda *_: (0,) * len(shape))


def call(kernel, outs, flops, nbytes, *args):
    return pl.pallas_call(
        kernel,
        out_shape=outs,
        compiler_params=pltpu.CompilerParams(vmem_limit_bytes=VMEM_LIMIT),
        cost_estimate=pl.CostEstimate(flops=flops, bytes_accessed=nbytes, transcendentals=0),
    )(*args)


def earlier(count):
    i = lax.broadcasted_iota(jnp.int32, (count, count), 0)
    j = lax.broadcasted_iota(jnp.int32, (count, count), 1)
    return (i < j).astype(jnp.bfloat16)


def pack_kernel(experts, capacity, assign_ref, tokens_ref, slots_ref, place_ref):
    tok_count = tokens_ref.shape[0]
    slot_total = slots_ref.shape[0]
    assign = assign_ref[...]
    ids = lax.broadcasted_iota(jnp.int32, (experts, tok_count), 0)
    onehot = (assign == ids).astype(jnp.float32)
    before = jnp.dot(
        onehot.astype(jnp.bfloat16), earlier(tok_count), preferred_element_type=jnp.float32
    )
    position = jnp.sum(before * onehot, axis=0, keepdims=True).astype(jnp.int32)
    slot_of = assign * capacity + position
    rows = lax.broadcasted_iota(jnp.int32, (slot_total, tok_count), 0)
    place = (rows == slot_of).astype(jnp.float32)
    taken = jnp.sum(place, axis=1, keepdims=True)
    place = place.astype(jnp.bfloat16)
    place_ref[...] = place
    packed = jnp.dot(place, tokens_ref[...], preferred_element_type=jnp.float32)
    slots_ref[...] = jnp.where(taken > 0.5, packed, EMPTY).astype(jnp.bfloat16)


def compact_kernel(slots_ref, gain_ref, centroid_ref, normed_ref, gate_ref, select_ref):
    slot_total = slots_ref.shape[0]
    rows = normed_ref.shape[0]
    first = (lax.broadcasted_iota(jnp.int32, (8, 128), 1) == 0).astype(jnp.bfloat16)
    mark = lax.dot_general(
        first, slots_ref[:, :128], (((1,), (1,)), ((), ())), preferred_element_type=jnp.float32
    )
    live = mark < 0.5 * EMPTY
    rank = jnp.dot(
        live.astype(jnp.bfloat16), earlier(slot_total), preferred_element_type=jnp.float32
    )
    rank = jnp.where(live, rank, -1.0)[:1].astype(jnp.int32)
    select = (lax.broadcasted_iota(jnp.int32, (rows, slot_total), 0) == rank).astype(jnp.bfloat16)
    select_ref[...] = select
    values = jnp.dot(select, slots_ref[...], preferred_element_type=jnp.float32)
    center = jnp.mean(values, axis=1, keepdims=True)
    shifted = values - center
    spread = jnp.mean(jnp.square(shifted), axis=1, keepdims=True)
    normed_ref[...] = (shifted * lax.rsqrt(spread + EPSILON) * gain_ref[...]).astype(jnp.bfloat16)
    score = jnp.sum(values * centroid_ref[...].astype(jnp.float32), axis=1, keepdims=True)
    gate = (1.0 / (1.0 + jnp.exp(-score))).astype(jnp.bfloat16).astype(jnp.float32)
    gate_ref[...] = jnp.broadcast_to(gate, gate_ref.shape)


def ffn_kernel(rows_ref, inner_ref, outer_ref, out_ref, total_ref):
    step = pl.program_id(0)

    @pl.when(step == 0)
    def _():
        total_ref[...] = jnp.zeros_like(total_ref)

    act = lax.dot_general(
        rows_ref[...], inner_ref[...], (((1,), (1,)), ((), ())), preferred_element_type=jnp.float32
    )
    hidden = jnp.maximum(act, 0.0).astype(jnp.bfloat16)
    total_ref[...] += jnp.dot(hidden, outer_ref[...], preferred_element_type=jnp.float32)

    @pl.when(step == pl.num_programs(0) - 1)
    def _():
        out_ref[...] = total_ref[...].astype(out_ref.dtype)


def ffn(rows, inner, outer):
    count, features = rows.shape
    units = inner.shape[0]
    tile = min(units, 256)
    return pl.pallas_call(
        ffn_kernel,
        out_shape=jax.ShapeDtypeStruct((count, features), jnp.bfloat16),
        grid=(units // tile,),
        in_specs=[
            whole((count, features)),
            pl.BlockSpec((tile, features), lambda i: (i, 0)),
            pl.BlockSpec((tile, features), lambda i: (i, 0)),
        ],
        out_specs=whole((count, features)),
        scratch_shapes=[pltpu.VMEM((count, features), jnp.float32)],
        compiler_params=pltpu.CompilerParams(vmem_limit_bytes=VMEM_LIMIT),
        cost_estimate=pl.CostEstimate(
            flops=4 * count * features * units,
            bytes_accessed=4 * units * features,
            transcendentals=0,
        ),
    )(rows, inner, outer)


def spread_kernel(parts, *refs):
    part_refs, gate_ref, select_ref, slots_ref = refs[:parts], refs[parts], refs[parts + 1], refs[parts + 2]
    total = part_refs[0][...].astype(jnp.float32)
    for ref in part_refs[1:]:
        total = total + ref[...].astype(jnp.float32)
    gated = (gate_ref[:, :1] * total).astype(jnp.bfloat16)
    slots_ref[...] = lax.dot_general(
        select_ref[...], gated, (((0,), (0,)), ((), ())), preferred_element_type=jnp.float32
    ).astype(jnp.bfloat16)


def final_kernel(tokens_ref, slots_ref, place_ref, out_ref):
    added = lax.dot_general(
        place_ref[...], slots_ref[...], (((0,), (0,)), ((), ())), preferred_element_type=jnp.float32
    )
    out_ref[...] = (tokens_ref[...].astype(jnp.float32) + added).astype(jnp.bfloat16)


def body(tokens, assignment, centroids, norm_gain, inner_weight, outer_weight):
    tok_count, features = tokens.shape
    experts = lax.axis_size("expert")
    groups = lax.axis_size("dp")
    capacity = 2 * tok_count // experts
    slot_total = experts * capacity
    shape = jax.ShapeDtypeStruct
    bf16 = jnp.bfloat16
    slot_bytes = 2 * slot_total * features
    move_flops = 2 * slot_total * tok_count * features
    outgoing, place = call(
        functools.partial(pack_kernel, experts, capacity),
        (shape((slot_total, features), bf16), shape((slot_total, tok_count), bf16)),
        move_flops,
        2 * slot_bytes,
        assignment.reshape(1, tok_count),
        tokens,
    )
    arrived = lax.all_to_all(outgoing, "expert", split_axis=0, concat_axis=0, tiled=True)
    normed, gate, select = call(
        compact_kernel,
        (
            shape((tok_count, features), bf16),
            shape((tok_count, 128), jnp.float32),
            shape((tok_count, slot_total), bf16),
        ),
        move_flops,
        2 * slot_bytes,
        arrived,
        norm_gain,
        centroids,
    )
    inner = inner_weight[0]
    outer = outer_weight[0]
    guests = []
    for k in range(1, groups):
        there = [(i, (i + k) % groups) for i in range(groups)]
        guests.append(lax.ppermute(normed, "dp", there))
    parts = [ffn(normed, inner, outer)]
    for k in range(1, groups):
        back = [((i + k) % groups, i) for i in range(groups)]
        parts.append(lax.ppermute(ffn(guests[k - 1], inner, outer), "dp", back))
    returning = call(
        functools.partial(spread_kernel, groups),
        shape((slot_total, features), bf16),
        move_flops,
        2 * slot_bytes,
        *parts,
        gate,
        select,
    )
    back_rows = lax.all_to_all(returning, "expert", split_axis=0, concat_axis=0, tiled=True)
    return call(
        final_kernel,
        shape((tok_count, features), bf16),
        move_flops,
        2 * slot_bytes,
        tokens,
        back_rows,
        place,
    )


def solution(mesh):
    in_specs = (
        P(("dp", "expert"), None),
        P(("dp", "expert")),
        P("expert", None),
        P("expert", None),
        P("expert", "dp", None),
        P("expert", "dp", None),
    )
    out_specs = P(("dp", "expert"), None)
    return jax.shard_map(body, mesh=mesh, in_specs=in_specs, out_specs=out_specs, check_vma=False)
```

```python
import functools

import jax
import jax.numpy as jnp
from jax import lax
from jax.experimental import pallas as pl
from jax.experimental.pallas import tpu as pltpu
from jax.sharding import PartitionSpec as P

EPSILON = 1e-05
EMPTY = 64.0
VMEM_LIMIT = 24 * 1024 * 1024
CHUNKS = 2


def whole(shape):
    return pl.BlockSpec(shape, lambda *_: (0,) * len(shape))


def call(kernel, outs, flops, nbytes, *args):
    return pl.pallas_call(
        kernel,
        out_shape=outs,
        compiler_params=pltpu.CompilerParams(vmem_limit_bytes=VMEM_LIMIT),
        cost_estimate=pl.CostEstimate(flops=flops, bytes_accessed=nbytes, transcendentals=0),
    )(*args)


def earlier(count):
    i = lax.broadcasted_iota(jnp.int32, (count, count), 0)
    j = lax.broadcasted_iota(jnp.int32, (count, count), 1)
    return (i < j).astype(jnp.bfloat16)


def fetch(sources, targets, sems):
    copies = [
        pltpu.make_async_copy(source, target, sems.at[i])
        for i, (source, target) in enumerate(zip(sources, targets))
    ]
    for copy in copies:
        copy.start()
    return copies


def pack_kernel(
    experts,
    capacity,
    assign_ref,
    tokens_ref,
    gain_ref,
    centroid_ref,
    slots_ref,
    place_ref,
    gain_out,
    centroid_out,
    assign_buf,
    tokens_buf,
    sems,
):
    tok_count = tokens_ref.shape[0]
    slot_total = slots_ref.shape[0]
    get_assign, *others = fetch(
        (assign_ref, tokens_ref, gain_ref, centroid_ref),
        (assign_buf, tokens_buf, gain_out, centroid_out),
        sems,
    )
    get_assign.wait()
    assign = assign_buf[...]
    ids = lax.broadcasted_iota(jnp.int32, (experts, tok_count), 0)
    onehot = (assign == ids).astype(jnp.float32)
    before = jnp.dot(
        onehot.astype(jnp.bfloat16), earlier(tok_count), preferred_element_type=jnp.float32
    )
    position = jnp.sum(before * onehot, axis=0, keepdims=True).astype(jnp.int32)
    slot_of = assign * capacity + position
    rows = lax.broadcasted_iota(jnp.int32, (slot_total, tok_count), 0)
    place = (rows == slot_of).astype(jnp.float32)
    taken = jnp.sum(place, axis=1, keepdims=True)
    place = place.astype(jnp.bfloat16)
    place_ref[...] = place
    for copy in others:
        copy.wait()
    packed = jnp.dot(place, tokens_buf[...], preferred_element_type=jnp.float32)
    slots_ref[...] = jnp.where(taken > 0.5, packed, EMPTY).astype(jnp.bfloat16)


def load_kernel(inner_ref, outer_ref, _, inner_out, outer_out, sems):
    for copy in fetch((inner_ref, outer_ref), (inner_out, outer_out), sems):
        copy.wait()


def compact_kernel(slots_ref, gain_ref, centroid_ref, *refs):
    chunk_refs, (normed_ref, gate_ref, select_ref) = refs[:-3], refs[-3:]
    slot_total = slots_ref.shape[0]
    rows = gate_ref.shape[0]
    first = (lax.broadcasted_iota(jnp.int32, (8, 128), 1) == 0).astype(jnp.bfloat16)
    mark = lax.dot_general(
        first, slots_ref[:, :128], (((1,), (1,)), ((), ())), preferred_element_type=jnp.float32
    )
    live = mark < 0.5 * EMPTY
    rank = jnp.dot(
        live.astype(jnp.bfloat16), earlier(slot_total), preferred_element_type=jnp.float32
    )
    rank = jnp.where(live, rank, -1.0)[:1].astype(jnp.int32)
    select = (lax.broadcasted_iota(jnp.int32, (rows, slot_total), 0) == rank).astype(jnp.bfloat16)
    select_ref[...] = select
    values = jnp.dot(select, slots_ref[...], preferred_element_type=jnp.float32)
    center = jnp.mean(values, axis=1, keepdims=True)
    shifted = values - center
    spread = jnp.mean(jnp.square(shifted), axis=1, keepdims=True)
    normed = (shifted * lax.rsqrt(spread + EPSILON) * gain_ref[...]).astype(jnp.bfloat16)
    normed_ref[...] = normed
    done = 0
    for ref in chunk_refs:
        ref[...] = normed[done : done + ref.shape[0]]
        done += ref.shape[0]
    score = jnp.sum(values * centroid_ref[...].astype(jnp.float32), axis=1, keepdims=True)
    gate = (1.0 / (1.0 + jnp.exp(-score))).astype(jnp.bfloat16).astype(jnp.float32)
    gate_ref[...] = jnp.broadcast_to(gate, gate_ref.shape)


def ffn_kernel(rows_ref, inner_ref, outer_ref, _, out_ref, total_ref):
    units = inner_ref.shape[0]
    tile = min(units, 1024)
    for start in range(0, units, tile):
        act = lax.dot_general(
            rows_ref[...],
            inner_ref[start : start + tile],
            (((1,), (1,)), ((), ())),
            preferred_element_type=jnp.float32,
        )
        hidden = jnp.maximum(act, 0.0).astype(jnp.bfloat16)
        more = jnp.dot(
            hidden, outer_ref[start : start + tile], preferred_element_type=jnp.float32
        )
        if start == 0:
            total_ref[...] = more
        else:
            total_ref[...] += more
    out_ref[...] = total_ref[...].astype(out_ref.dtype)


def ffn(rows, inner, outer, after):
    count, features = rows.shape
    units = inner.shape[0]
    return pl.pallas_call(
        ffn_kernel,
        out_shape=jax.ShapeDtypeStruct((count, features), jnp.bfloat16),
        in_specs=[pl.BlockSpec(memory_space=pltpu.VMEM)] * 3 + [pl.BlockSpec(memory_space=pl.ANY)],
        out_specs=pl.BlockSpec(memory_space=pltpu.VMEM),
        scratch_shapes=[pltpu.VMEM((count, features), jnp.float32)],
        compiler_params=pltpu.CompilerParams(vmem_limit_bytes=VMEM_LIMIT),
        cost_estimate=pl.CostEstimate(
            flops=4 * max(count, 256) * features * units,
            bytes_accessed=4 * count * features,
            transcendentals=0,
        ),
    )(rows, inner, outer, after)


def spread_kernel(groups, *refs):
    gate_ref, select_ref, slots_ref = refs[-3:]
    chunks = (len(refs) - 4) // (groups - 1)
    total = refs[0][...].astype(jnp.float32)
    for g in range(1, groups):
        first = 1 + (g - 1) * chunks
        rows = [ref[...].astype(jnp.float32) for ref in refs[first : first + chunks]]
        total = total + jnp.concatenate(rows, axis=0)
    gated = (gate_ref[:, :1] * total).astype(jnp.bfloat16)
    slots_ref[...] = lax.dot_general(
        select_ref[...], gated, (((0,), (0,)), ((), ())), preferred_element_type=jnp.float32
    ).astype(jnp.bfloat16)


def final_kernel(tokens_ref, slots_ref, place_ref, out_ref):
    added = lax.dot_general(
        place_ref[...], slots_ref[...], (((0,), (0,)), ((), ())), preferred_element_type=jnp.float32
    )
    out_ref[...] = (tokens_ref[...].astype(jnp.float32) + added).astype(jnp.bfloat16)


def body(tokens, assignment, centroids, norm_gain, inner_weight, outer_weight):
    tok_count, features = tokens.shape
    experts = lax.axis_size("expert")
    groups = lax.axis_size("dp")
    capacity = 2 * tok_count // experts
    slot_total = experts * capacity
    shape = jax.ShapeDtypeStruct
    bf16 = jnp.bfloat16
    slot_bytes = 2 * slot_total * features
    move_flops = 2 * slot_total * tok_count * features
    local = pl.BlockSpec(memory_space=pltpu.VMEM)
    far = pl.BlockSpec(memory_space=pltpu.HBM)
    stay = lambda x: pltpu.with_memory_space_constraint(x, pltpu.HBM)
    outgoing, place, gain, centroid = pl.pallas_call(
        functools.partial(pack_kernel, experts, capacity),
        out_shape=(
            shape((slot_total, features), bf16),
            shape((slot_total, tok_count), bf16),
            pltpu.VMEM((1, features), jnp.float32),
            pltpu.VMEM((1, features), bf16),
        ),
        in_specs=[far] * 4,
        out_specs=(local,) * 4,
        scratch_shapes=[
            pltpu.VMEM((1, tok_count), jnp.int32),
            pltpu.VMEM((tok_count, features), bf16),
            pltpu.SemaphoreType.DMA((4,)),
        ],
        compiler_params=pltpu.CompilerParams(vmem_limit_bytes=VMEM_LIMIT),
        cost_estimate=pl.CostEstimate(
            flops=move_flops, bytes_accessed=2 * slot_bytes, transcendentals=0
        ),
    )(stay(assignment.reshape(1, tok_count)), stay(tokens), stay(norm_gain), stay(centroids))
    arrived = lax.all_to_all(outgoing, "expert", split_axis=0, concat_axis=0, tiled=True)
    half = tok_count // CHUNKS
    *chunks, normed, gate, select = pl.pallas_call(
        compact_kernel,
        out_shape=(shape((half, features), bf16),) * CHUNKS
        + (
            shape((tok_count, features), bf16),
            shape((tok_count, 128), jnp.float32),
            shape((tok_count, slot_total), bf16),
        ),
        in_specs=[local] * 3,
        out_specs=(local,) * (CHUNKS + 3),
        compiler_params=pltpu.CompilerParams(vmem_limit_bytes=VMEM_LIMIT),
        cost_estimate=pl.CostEstimate(
            flops=move_flops, bytes_accessed=2 * slot_bytes, transcendentals=0
        ),
    )(arrived, gain, centroid)
    weights = (inner_weight[0], outer_weight[0])
    inner, outer = pl.pallas_call(
        load_kernel,
        out_shape=tuple(pltpu.VMEM(w.shape, bf16) for w in weights),
        in_specs=[far, far, pl.BlockSpec(memory_space=pl.ANY)],
        out_specs=(local, local),
        scratch_shapes=[pltpu.SemaphoreType.DMA((2,))],
        compiler_params=pltpu.CompilerParams(vmem_limit_bytes=VMEM_LIMIT),
        cost_estimate=pl.CostEstimate(
            flops=0, bytes_accessed=4 * weights[0].size, transcendentals=0
        ),
    )(*map(stay, weights), gate)
    guests = []
    for k in range(1, groups):
        there = [(i, (i + k) % groups) for i in range(groups)]
        guests.append([lax.ppermute(rows, "dp", there) for rows in chunks])
    visits = []
    for k in range(1, groups):
        back = [((i + k) % groups, i) for i in range(groups)]
        sums = [ffn(rows, inner, outer, gate) for rows in guests[k - 1]]
        visits.append([lax.ppermute(rows, "dp", back) for rows in sums])
    parts = [ffn(normed, inner, outer, sums[-1])]
    for visit in visits:
        parts += visit
    returning = call(
        functools.partial(spread_kernel, groups),
        shape((slot_total, features), bf16),
        move_flops,
        2 * slot_bytes,
        *parts,
        gate,
        select,
    )
    back_rows = lax.all_to_all(returning, "expert", split_axis=0, concat_axis=0, tiled=True)
    return call(
        final_kernel,
        shape((tok_count, features), bf16),
        move_flops,
        2 * slot_bytes,
        tokens,
        back_rows,
        place,
    )


def solution(mesh):
    in_specs = (
        P(("dp", "expert"), None),
        P(("dp", "expert")),
        P("expert", None),
        P("expert", None),
        P("expert", "dp", None),
        P("expert", "dp", None),
    )
    out_specs = P(("dp", "expert"), None)
    return jax.shard_map(body, mesh=mesh, in_specs=in_specs, out_specs=out_specs, check_vma=False)
```

```python
import functools

import jax
import jax.numpy as jnp
from jax import lax
from jax.experimental import pallas as pl
from jax.experimental.pallas import tpu as pltpu
from jax.sharding import PartitionSpec as P

EPSILON = 1e-05
EMPTY = 64.0
VMEM_LIMIT = 24 * 1024 * 1024
FIRST_SHARE = 9
LOCAL = pl.BlockSpec(memory_space=pltpu.VMEM)
FAR = pl.BlockSpec(memory_space=pltpu.HBM)
ANYWHERE = pl.BlockSpec(memory_space=pl.ANY)
BF16 = jnp.bfloat16
F32 = jnp.float32


def shape(*dims, dtype=BF16):
    return jax.ShapeDtypeStruct(dims, dtype)


def call(kernel, outs, args, flops, nbytes, in_specs=None, scratch=()):
    return pl.pallas_call(
        kernel,
        out_shape=tuple(outs),
        in_specs=[LOCAL] * len(args) if in_specs is None else in_specs,
        out_specs=(LOCAL,) * len(outs),
        scratch_shapes=list(scratch),
        compiler_params=pltpu.CompilerParams(vmem_limit_bytes=VMEM_LIMIT),
        cost_estimate=pl.CostEstimate(flops=flops, bytes_accessed=nbytes, transcendentals=0),
    )(*args)


def stay(array):
    return pltpu.with_memory_space_constraint(array, pltpu.HBM)


def fetch(sources, targets, sems):
    copies = [
        pltpu.make_async_copy(source, target, sems.at[i])
        for i, (source, target) in enumerate(zip(sources, targets))
    ]
    for copy in copies:
        copy.start()
    return copies


def earlier(count):
    i = lax.broadcasted_iota(jnp.int32, (count, count), 0)
    j = lax.broadcasted_iota(jnp.int32, (count, count), 1)
    return (i < j).astype(BF16)


def dot(a, b, dims=((1,), (0,))):
    return lax.dot_general(a, b, (dims, ((), ())), preferred_element_type=F32)


def put_slots(slots, refs, capacity):
    if len(refs) == 1:
        refs[0][...] = slots
        return
    for block in range(slots.shape[0] // capacity):
        row = block // 2 * capacity
        refs[block % 2][row : row + capacity] = slots[block * capacity : (block + 1) * capacity]


def get_blocks(refs):
    return jnp.concatenate([ref[...] for ref in refs], axis=0)


def pair_kernel(capacity, stay_ref, crossed_ref, _, *pair_refs):
    pairs = stay_ref.shape[0] // capacity
    for i in range(pairs):
        source = slice(i * capacity, (i + 1) * capacity)
        ref = pair_refs[i % len(pair_refs)]
        row = i // len(pair_refs) * 2 * capacity
        ref[row : row + capacity] = stay_ref[source]
        ref[row + capacity : row + 2 * capacity] = crossed_ref[source]


def pack_kernel(targets, experts, capacity, cut, *refs):
    assign_ref, tokens_ref, gain_ref, centroid_ref = refs[:4]
    halves = refs[4 : 4 + targets], refs[4 + targets : 4 + 2 * targets]
    place_ref, gain_out, centroid_out, assign_buf, tokens_buf, sems = refs[4 + 2 * targets :]
    tok_count = tokens_ref.shape[0]
    slot_total = place_ref.shape[0]
    get_assign, *others = fetch(
        (assign_ref, tokens_ref, gain_ref, centroid_ref),
        (assign_buf, tokens_buf, gain_out, centroid_out),
        sems,
    )
    get_assign.wait()
    assign = assign_buf[...]
    if targets == 2:
        assign = assign ^ lax.axis_index("expert")
    ids = lax.broadcasted_iota(jnp.int32, (experts, tok_count), 0)
    onehot = (assign == ids).astype(F32)
    before = dot(onehot.astype(BF16), earlier(tok_count))
    position = jnp.sum(before * onehot, axis=0, keepdims=True).astype(jnp.int32)
    rows = lax.broadcasted_iota(jnp.int32, (slot_total, tok_count), 0)
    place_ref[...] = (rows == assign_buf[...] * capacity + position).astype(F32).astype(BF16)
    place = (rows == assign * capacity + position).astype(F32)
    taken = jnp.sum(place, axis=1, keepdims=True)
    place = place.astype(BF16)
    for copy in others:
        copy.wait()
    packed = dot(place, tokens_buf[...])
    packed = jnp.where(taken > 0.5, packed, EMPTY).astype(BF16)
    put_slots(packed[:, :cut], halves[0], capacity)
    put_slots(packed[:, cut:], halves[1], capacity)


def load_kernel(inner_ref, outer_ref, _, inner_out, outer_out, sems):
    for copy in fetch((inner_ref, outer_ref), (inner_out, outer_out), sems):
        copy.wait()


def first_kernel(*refs):
    block_refs, (rows_ref, select_ref) = refs[:-2], refs[-2:]
    slots = get_blocks(block_refs)
    first = (lax.broadcasted_iota(jnp.int32, (8, 128), 1) == 0).astype(BF16)
    live = dot(first, slots[:, :128], ((1,), (1,))) < 0.5 * EMPTY
    rank = dot(live.astype(BF16), earlier(slots.shape[0]))
    rank = jnp.where(live, rank, -1.0)[:1].astype(jnp.int32)
    ids = lax.broadcasted_iota(jnp.int32, select_ref.shape, 0)
    select = (ids == rank).astype(BF16)
    select_ref[...] = select
    rows_ref[...] = dot(select, slots).astype(BF16)


def second_kernel(*refs):
    block_refs, (select_ref, rows_ref) = refs[:-2], refs[-2:]
    rows_ref[...] = dot(select_ref[...], get_blocks(block_refs)).astype(BF16)


def normalize(left, right, gain):
    count = left.shape[1] + right.shape[1]
    center = (
        jnp.sum(left, axis=1, keepdims=True) + jnp.sum(right, axis=1, keepdims=True)
    ) / count
    left, right = left - center, right - center
    spread = (
        jnp.sum(jnp.square(left), axis=1, keepdims=True)
        + jnp.sum(jnp.square(right), axis=1, keepdims=True)
    ) / count
    scale = lax.rsqrt(spread + EPSILON)
    cut = left.shape[1]
    left = (left * scale * gain[:, :cut]).astype(BF16)
    right = (right * scale * gain[:, cut:]).astype(BF16)
    return jnp.concatenate([left, right], axis=1)


def project(normed_ref, inner_ref, hidden_ref):
    units = inner_ref.shape[0]
    tile = min(units, 1024)
    for start in range(0, units, tile):
        act = dot(normed_ref[...], inner_ref[start : start + tile], ((1,), (1,)))
        hidden_ref[:, start : start + tile] = jnp.maximum(act, 0.0).astype(BF16)


def own_kernel(
    left_ref,
    right_ref,
    gain_ref,
    centroid_ref,
    inner_ref,
    outer_ref,
    left_out,
    right_out,
    gate_ref,
    normed_ref,
    hidden_ref,
):
    cut = left_ref.shape[1]
    left, right = left_ref[...].astype(F32), right_ref[...].astype(F32)
    centroid = centroid_ref[...].astype(F32)
    score = jnp.sum(left * centroid[:, :cut], axis=1, keepdims=True)
    score = score + jnp.sum(right * centroid[:, cut:], axis=1, keepdims=True)
    gate = (1.0 / (1.0 + jnp.exp(-score))).astype(BF16).astype(F32)
    gate_ref[...] = jnp.broadcast_to(gate, gate_ref.shape)
    normed_ref[...] = normalize(left, right, gain_ref[...])
    project(normed_ref, inner_ref, hidden_ref)
    cut = left_out.shape[1]
    left_out[...] = dot(hidden_ref[...], outer_ref[:, :cut]).astype(BF16)
    right_out[...] = dot(hidden_ref[...], outer_ref[:, cut:]).astype(BF16)


def guest_kernel(
    left_ref, right_ref, gain_ref, inner_ref, outer_ref, left_out, hidden_ref, normed_ref
):
    cut = left_out.shape[1]
    normed_ref[...] = normalize(
        left_ref[...].astype(F32), right_ref[...].astype(F32), gain_ref[...]
    )
    project(normed_ref, inner_ref, hidden_ref)
    left_out[...] = dot(hidden_ref[...], outer_ref[:, :cut]).astype(BF16)


def rest_kernel(hidden_ref, outer_ref, right_out):
    cut = outer_ref.shape[1] - right_out.shape[1]
    right_out[...] = dot(hidden_ref[...], outer_ref[:, cut:]).astype(BF16)


def spread_kernel(groups, capacity, relative, *refs):
    gate_ref, select_ref, slots_ref = refs[2 * groups :]
    sums = []
    for part_refs in (refs[:groups], refs[groups : 2 * groups]):
        total = part_refs[0][...].astype(F32)
        for ref in part_refs[1:]:
            total = total + ref[...].astype(F32)
        sums.append((gate_ref[:, :1] * total).astype(BF16))
    slots = dot(select_ref[...], jnp.concatenate(sums, axis=1), ((0,), (0,))).astype(BF16)
    if not relative:
        slots_ref[...] = slots
        return
    me = lax.axis_index("expert")
    for j in range(slots.shape[0] // capacity):
        row = pl.multiple_of((me ^ j) * capacity, capacity)
        slots_ref[pl.ds(row, capacity)] = slots[j * capacity : (j + 1) * capacity]


def final_kernel(tokens_ref, slots_ref, place_ref, out_ref):
    added = dot(place_ref[...], slots_ref[...], ((0,), (0,)))
    out_ref[...] = (tokens_ref[...].astype(F32) + added).astype(BF16)


def swap(array, axis_mask, experts):
    return lax.ppermute(array, "expert", [(i, i ^ axis_mask) for i in range(experts)])


def pair(stay, crossed, targets, capacity, after):
    rows, width = stay.shape
    return call(
        functools.partial(pair_kernel, capacity),
        [shape(2 * rows // targets, width) for _ in range(targets)],
        [stay, crossed, after],
        0,
        8 * rows * width,
        [LOCAL, LOCAL, ANYWHERE],
    )


def exchange(halves, experts, capacity, after=None):
    crossed = swap(halves[1], 1, experts)
    after = halves[0] if after is None else after
    blocks = list(pair(halves[0], crossed, experts // 2, capacity, after))
    for j in reversed(range(1, experts // 2)):
        blocks[j] = swap(blocks[j], 2 * j, experts)
    return blocks


def together(rows):
    return lax.all_to_all(rows, "expert", split_axis=0, concat_axis=0, tiled=True)


def body(tokens, assignment, centroids, norm_gain, inner_weight, outer_weight):
    tok_count, features = tokens.shape
    experts = lax.axis_size("expert")
    groups = lax.axis_size("dp")
    capacity = 2 * tok_count // experts
    slot_total = experts * capacity
    units = inner_weight.shape[1]
    targets = 2 if capacity % 16 == 0 and experts & (experts - 1) == 0 and experts >= 8 else 1
    cut = features // 128 * FIRST_SHARE // 16 * 128
    widths = (cut, features - cut)
    back_cut = (features // 128 + 1) // 2 * 128
    back_widths = (back_cut, features - back_cut)
    move_flops = slot_total * tok_count * features
    half_bytes = 2 * slot_total * features
    *packed, place, gain, centroid = call(
        functools.partial(pack_kernel, targets, experts, capacity, cut),
        [shape(slot_total // targets, w) for w in widths for _ in range(targets)]
        + [
            shape(slot_total, tok_count),
            pltpu.VMEM((1, features), F32),
            pltpu.VMEM((1, features), BF16),
        ],
        [stay(a) for a in (assignment.reshape(1, tok_count), tokens, norm_gain, centroids)],
        2 * move_flops,
        2 * half_bytes,
        [FAR] * 4,
        [
            pltpu.VMEM((1, tok_count), jnp.int32),
            pltpu.VMEM((tok_count, features), BF16),
            pltpu.SemaphoreType.DMA((4,)),
        ],
    )
    if targets == 2:
        first = exchange(packed[:targets], experts, capacity)
        second = exchange(packed[targets:], experts, capacity, first[1])
    else:
        first, second = [together(packed[0])], [together(packed[1])]
    rows, select = call(
        first_kernel,
        [shape(tok_count, cut), shape(tok_count, slot_total)],
        first,
        move_flops,
        half_bytes,
    )
    there = [[(i, (i + k) % groups) for i in range(groups)] for k in range(groups)]
    back = [[(t, s) for s, t in pairs] for pairs in there]
    left_guests = [lax.ppermute(rows, "dp", there[k]) for k in range(1, groups)]
    weights = (inner_weight[0], outer_weight[0])
    inner, outer = call(
        load_kernel,
        [pltpu.VMEM(w.shape, BF16) for w in weights],
        [stay(w) for w in weights] + [select],
        0,
        8 * units * features,
        [FAR, FAR, ANYWHERE],
        [pltpu.SemaphoreType.DMA((2,))],
    )
    (right_rows,) = call(
        second_kernel,
        [shape(tok_count, widths[1])],
        [*second, select],
        move_flops,
        half_bytes,
    )
    right_guests = [lax.ppermute(right_rows, "dp", there[k]) for k in range(1, groups)]
    ffn_flops = 4 * 2 * tok_count * units * features
    wide = [pltpu.VMEM((tok_count, features), BF16)]
    own_left, own_right, gate = call(
        own_kernel,
        [shape(tok_count, w) for w in back_widths] + [shape(tok_count, 128, dtype=F32)],
        [rows, right_rows, gain, centroid, inner, outer],
        ffn_flops,
        half_bytes,
        scratch=wide + [pltpu.VMEM((tok_count, units), BF16)],
    )
    left_parts, right_parts = [own_left], [own_right]
    for k in range(1, groups):
        left_part, hidden = call(
            guest_kernel,
            [shape(tok_count, back_cut), shape(tok_count, units)],
            [left_guests[k - 1], right_guests[k - 1], gain, inner, outer],
            ffn_flops * 3 // 4,
            half_bytes,
            scratch=wide,
        )
        left_parts.append(lax.ppermute(left_part, "dp", back[k]))
        (right_part,) = call(
            rest_kernel,
            [shape(tok_count, back_widths[1])],
            [hidden, outer],
            ffn_flops // 4,
            half_bytes,
        )
        right_parts.append(lax.ppermute(right_part, "dp", back[k]))
    (leaving,) = call(
        functools.partial(spread_kernel, groups, capacity, targets == 2),
        [shape(slot_total, features)],
        [*left_parts, *right_parts, gate, select],
        2 * move_flops,
        2 * half_bytes,
    )
    (out,) = call(
        final_kernel,
        [shape(tok_count, features)],
        [tokens, together(leaving), place],
        2 * move_flops,
        2 * half_bytes,
    )
    return out


def solution(mesh):
    in_specs = (
        P(("dp", "expert"), None),
        P(("dp", "expert")),
        P("expert", None),
        P("expert", None),
        P("expert", "dp", None),
        P("expert", "dp", None),
    )
    out_specs = P(("dp", "expert"), None)
    return jax.shard_map(body, mesh=mesh, in_specs=in_specs, out_specs=out_specs, check_vma=False)
```

```python
import functools

import jax
import jax.numpy as jnp
from jax import lax
from jax.experimental import pallas as pl
from jax.experimental.pallas import tpu as pltpu
from jax.sharding import PartitionSpec as P

EPSILON = 1e-05
EMPTY = 64.0
VMEM_LIMIT = 24 * 1024 * 1024
FIRST_SHARE = 9
LOCAL = pl.BlockSpec(memory_space=pltpu.VMEM)
FAR = pl.BlockSpec(memory_space=pltpu.HBM)
ANYWHERE = pl.BlockSpec(memory_space=pl.ANY)
BF16 = jnp.bfloat16
F32 = jnp.float32


def shape(*dims, dtype=BF16):
    return jax.ShapeDtypeStruct(dims, dtype)


def call(kernel, outs, args, flops, nbytes, in_specs=None, scratch=()):
    return pl.pallas_call(
        kernel,
        out_shape=tuple(outs),
        in_specs=[LOCAL] * len(args) if in_specs is None else in_specs,
        out_specs=(LOCAL,) * len(outs),
        scratch_shapes=list(scratch),
        compiler_params=pltpu.CompilerParams(vmem_limit_bytes=VMEM_LIMIT),
        cost_estimate=pl.CostEstimate(flops=flops, bytes_accessed=nbytes, transcendentals=0),
    )(*args)


def stay(array):
    return pltpu.with_memory_space_constraint(array, pltpu.HBM)


def fetch(sources, targets, sems):
    copies = [
        pltpu.make_async_copy(source, target, sems.at[i])
        for i, (source, target) in enumerate(zip(sources, targets))
    ]
    for copy in copies:
        copy.start()
    return copies


def earlier(count):
    i = lax.broadcasted_iota(jnp.int32, (count, count), 0)
    j = lax.broadcasted_iota(jnp.int32, (count, count), 1)
    return (i < j).astype(BF16)


def dot(a, b, dims=((1,), (0,))):
    return lax.dot_general(a, b, (dims, ((), ())), preferred_element_type=F32)


def put_slots(slots, refs, capacity):
    if len(refs) == 1:
        refs[0][...] = slots
        return
    for block in range(slots.shape[0] // capacity):
        row = block // 2 * capacity
        refs[block % 2][row : row + capacity] = slots[block * capacity : (block + 1) * capacity]


def get_blocks(refs):
    return jnp.concatenate([ref[...] for ref in refs], axis=0)


def pair_kernel(capacity, stay_ref, crossed_ref, _, *pair_refs):
    pairs = stay_ref.shape[0] // capacity
    for i in range(pairs):
        source = slice(i * capacity, (i + 1) * capacity)
        ref = pair_refs[i % len(pair_refs)]
        row = i // len(pair_refs) * 2 * capacity
        ref[row : row + capacity] = stay_ref[source]
        ref[row + capacity : row + 2 * capacity] = crossed_ref[source]


def pack_kernel(targets, experts, capacity, cut, *refs):
    assign_ref, tokens_ref, gain_ref, centroid_ref = refs[:4]
    halves = refs[4 : 4 + targets], refs[4 + targets : 4 + 2 * targets]
    place_ref, gain_out, centroid_out, assign_buf, tokens_buf, sems = refs[4 + 2 * targets :]
    tok_count = tokens_ref.shape[0]
    slot_total = place_ref.shape[0]
    get_assign, *others = fetch(
        (assign_ref, tokens_ref, gain_ref, centroid_ref),
        (assign_buf, tokens_buf, gain_out, centroid_out),
        sems,
    )
    get_assign.wait()
    assign = assign_buf[...]
    if targets == 2:
        assign = assign ^ lax.axis_index("expert")
    ids = lax.broadcasted_iota(jnp.int32, (experts, tok_count), 0)
    onehot = (assign == ids).astype(F32)
    before = dot(onehot.astype(BF16), earlier(tok_count))
    position = jnp.sum(before * onehot, axis=0, keepdims=True).astype(jnp.int32)
    rows = lax.broadcasted_iota(jnp.int32, (slot_total, tok_count), 0)
    place_ref[...] = (rows == assign_buf[...] * capacity + position).astype(F32).astype(BF16)
    place = (rows == assign * capacity + position).astype(F32)
    taken = jnp.sum(place, axis=1, keepdims=True)
    place = place.astype(BF16)
    for copy in others:
        copy.wait()
    packed = dot(place, tokens_buf[...])
    packed = jnp.where(taken > 0.5, packed, EMPTY).astype(BF16)
    put_slots(packed[:, :cut], halves[0], capacity)
    put_slots(packed[:, cut:], halves[1], capacity)


def load_kernel(inner_ref, outer_ref, _, inner_out, outer_out, sems):
    for copy in fetch((inner_ref, outer_ref), (inner_out, outer_out), sems):
        copy.wait()


def first_kernel(*refs):
    block_refs, (rows_ref, select_ref) = refs[:-2], refs[-2:]
    slots = get_blocks(block_refs)
    first = (lax.broadcasted_iota(jnp.int32, (8, 128), 1) == 0).astype(BF16)
    live = dot(first, slots[:, :128], ((1,), (1,))) < 0.5 * EMPTY
    rank = dot(live.astype(BF16), earlier(slots.shape[0]))
    rank = jnp.where(live, rank, -1.0)[:1].astype(jnp.int32)
    ids = lax.broadcasted_iota(jnp.int32, select_ref.shape, 0)
    select = (ids == rank).astype(BF16)
    select_ref[...] = select
    rows_ref[...] = dot(select, slots).astype(BF16)


def second_kernel(*refs):
    block_refs, (select_ref, rows_ref) = refs[:-2], refs[-2:]
    rows_ref[...] = dot(select_ref[...], get_blocks(block_refs)).astype(BF16)


def normalize(left, right, gain):
    count = left.shape[1] + right.shape[1]
    center = (
        jnp.sum(left, axis=1, keepdims=True) + jnp.sum(right, axis=1, keepdims=True)
    ) / count
    left, right = left - center, right - center
    spread = (
        jnp.sum(jnp.square(left), axis=1, keepdims=True)
        + jnp.sum(jnp.square(right), axis=1, keepdims=True)
    ) / count
    scale = lax.rsqrt(spread + EPSILON)
    cut = left.shape[1]
    left = (left * scale * gain[:, :cut]).astype(BF16)
    right = (right * scale * gain[:, cut:]).astype(BF16)
    return jnp.concatenate([left, right], axis=1)


def project(normed_ref, inner_ref, hidden_ref):
    units = inner_ref.shape[0]
    tile = min(units, 1024)
    for start in range(0, units, tile):
        act = dot(normed_ref[...], inner_ref[start : start + tile], ((1,), (1,)))
        hidden_ref[:, start : start + tile] = jnp.maximum(act, 0.0).astype(BF16)


def own_kernel(
    left_ref,
    right_ref,
    gain_ref,
    centroid_ref,
    inner_ref,
    outer_ref,
    left_out,
    right_out,
    gate_ref,
    normed_ref,
    hidden_ref,
):
    cut = left_ref.shape[1]
    left, right = left_ref[...].astype(F32), right_ref[...].astype(F32)
    centroid = centroid_ref[...].astype(F32)
    score = jnp.sum(left * centroid[:, :cut], axis=1, keepdims=True)
    score = score + jnp.sum(right * centroid[:, cut:], axis=1, keepdims=True)
    gate = (1.0 / (1.0 + jnp.exp(-score))).astype(BF16).astype(F32)
    gate_ref[...] = jnp.broadcast_to(gate, gate_ref.shape)
    normed_ref[...] = normalize(left, right, gain_ref[...])
    project(normed_ref, inner_ref, hidden_ref)
    cut = left_out.shape[1]
    left_out[...] = dot(hidden_ref[...], outer_ref[:, :cut]).astype(BF16)
    right_out[...] = dot(hidden_ref[...], outer_ref[:, cut:]).astype(BF16)


def guest_kernel(
    left_ref, right_ref, gain_ref, inner_ref, outer_ref, left_out, hidden_ref, normed_ref
):
    cut = left_out.shape[1]
    normed_ref[...] = normalize(
        left_ref[...].astype(F32), right_ref[...].astype(F32), gain_ref[...]
    )
    project(normed_ref, inner_ref, hidden_ref)
    left_out[...] = dot(hidden_ref[...], outer_ref[:, :cut]).astype(BF16)


def rest_kernel(hidden_ref, outer_ref, right_out):
    cut = outer_ref.shape[1] - right_out.shape[1]
    right_out[...] = dot(hidden_ref[...], outer_ref[:, cut:]).astype(BF16)


def spread_kernel(groups, capacity, relative, *refs):
    gate_ref, select_ref, slots_ref = refs[2 * groups :]
    sums = []
    for part_refs in (refs[:groups], refs[groups : 2 * groups]):
        total = part_refs[0][...].astype(F32)
        for ref in part_refs[1:]:
            total = total + ref[...].astype(F32)
        sums.append((gate_ref[:, :1] * total).astype(BF16))
    slots = dot(select_ref[...], jnp.concatenate(sums, axis=1), ((0,), (0,))).astype(BF16)
    if not relative:
        slots_ref[...] = slots
        return
    me = lax.axis_index("expert")
    for j in range(slots.shape[0] // capacity):
        row = pl.multiple_of((me ^ j) * capacity, capacity)
        slots_ref[pl.ds(row, capacity)] = slots[j * capacity : (j + 1) * capacity]


def final_kernel(tokens_ref, slots_ref, place_ref, out_ref):
    added = dot(place_ref[...], slots_ref[...], ((0,), (0,)))
    out_ref[...] = (tokens_ref[...].astype(F32) + added).astype(BF16)


def swap(array, axis_mask, experts):
    return lax.ppermute(array, "expert", [(i, i ^ axis_mask) for i in range(experts)])


def pair(stay, crossed, targets, capacity, after):
    rows, width = stay.shape
    return call(
        functools.partial(pair_kernel, capacity),
        [shape(2 * rows // targets, width) for _ in range(targets)],
        [stay, crossed, after],
        0,
        8 * rows * width,
        [LOCAL, LOCAL, ANYWHERE],
    )


def exchange(halves, experts, capacity, after=None):
    crossed = swap(halves[1], 1, experts)
    after = halves[0] if after is None else after
    blocks = list(pair(halves[0], crossed, experts // 2, capacity, after))
    for j in reversed(range(1, experts // 2)):
        blocks[j] = swap(blocks[j], 2 * j, experts)
    return blocks


def together(rows):
    return lax.all_to_all(rows, "expert", split_axis=0, concat_axis=0, tiled=True)


def body(tokens, assignment, centroids, norm_gain, inner_weight, outer_weight):
    tok_count, features = tokens.shape
    experts = lax.axis_size("expert")
    groups = lax.axis_size("dp")
    capacity = 2 * tok_count // experts
    slot_total = experts * capacity
    units = inner_weight.shape[1]
    targets = 2 if capacity % 16 == 0 and experts & (experts - 1) == 0 and experts >= 8 else 1
    cut = features // 128 * FIRST_SHARE // 16 * 128
    widths = (cut, features - cut)
    back_cut = (features // 128 * 3 + 3) // 4 * 128
    back_widths = (back_cut, features - back_cut)
    move_flops = slot_total * tok_count * features
    half_bytes = 2 * slot_total * features
    *packed, place, gain, centroid = call(
        functools.partial(pack_kernel, targets, experts, capacity, cut),
        [shape(slot_total // targets, w) for w in widths for _ in range(targets)]
        + [
            shape(slot_total, tok_count),
            pltpu.VMEM((1, features), F32),
            pltpu.VMEM((1, features), BF16),
        ],
        [stay(a) for a in (assignment.reshape(1, tok_count), tokens, norm_gain, centroids)],
        2 * move_flops,
        2 * half_bytes,
        [FAR] * 4,
        [
            pltpu.VMEM((1, tok_count), jnp.int32),
            pltpu.VMEM((tok_count, features), BF16),
            pltpu.SemaphoreType.DMA((4,)),
        ],
    )
    if targets == 2:
        first = exchange(packed[:targets], experts, capacity)
        second = exchange(packed[targets:], experts, capacity, first[experts // 4])
    else:
        first, second = [together(packed[0])], [together(packed[1])]
    rows, select = call(
        first_kernel,
        [shape(tok_count, cut), shape(tok_count, slot_total)],
        first,
        move_flops,
        half_bytes,
    )
    there = [[(i, (i + k) % groups) for i in range(groups)] for k in range(groups)]
    back = [[(t, s) for s, t in pairs] for pairs in there]
    left_guests = [lax.ppermute(rows, "dp", there[k]) for k in range(1, groups)]
    weights = (inner_weight[0], outer_weight[0])
    inner, outer = call(
        load_kernel,
        [pltpu.VMEM(w.shape, BF16) for w in weights],
        [stay(w) for w in weights] + [select],
        0,
        8 * units * features,
        [FAR, FAR, ANYWHERE],
        [pltpu.SemaphoreType.DMA((2,))],
    )
    (right_rows,) = call(
        second_kernel,
        [shape(tok_count, widths[1])],
        [*second, select],
        move_flops,
        half_bytes,
    )
    right_guests = [lax.ppermute(right_rows, "dp", there[k]) for k in range(1, groups)]
    ffn_flops = 4 * 2 * tok_count * units * features
    wide = [pltpu.VMEM((tok_count, features), BF16)]
    own_left, own_right, gate = call(
        own_kernel,
        [shape(tok_count, w) for w in back_widths] + [shape(tok_count, 128, dtype=F32)],
        [rows, right_rows, gain, centroid, inner, outer],
        ffn_flops,
        half_bytes,
        scratch=wide + [pltpu.VMEM((tok_count, units), BF16)],
    )
    left_parts, right_parts = [own_left], [own_right]
    for k in range(1, groups):
        left_part, hidden = call(
            guest_kernel,
            [shape(tok_count, back_cut), shape(tok_count, units)],
            [left_guests[k - 1], right_guests[k - 1], gain, inner, outer],
            ffn_flops * 3 // 4,
            half_bytes,
            scratch=wide,
        )
        left_parts.append(lax.ppermute(left_part, "dp", back[k]))
        (right_part,) = call(
            rest_kernel,
            [shape(tok_count, back_widths[1])],
            [hidden, outer],
            ffn_flops // 4,
            half_bytes,
        )
        right_parts.append(lax.ppermute(right_part, "dp", back[k]))
    (leaving,) = call(
        functools.partial(spread_kernel, groups, capacity, targets == 2),
        [shape(slot_total, features)],
        [*left_parts, *right_parts, gate, select],
        2 * move_flops,
        2 * half_bytes,
    )
    (out,) = call(
        final_kernel,
        [shape(tok_count, features)],
        [tokens, together(leaving), place],
        2 * move_flops,
        2 * half_bytes,
    )
    return out


def solution(mesh):
    in_specs = (
        P(("dp", "expert"), None),
        P(("dp", "expert")),
        P("expert", None),
        P("expert", None),
        P("expert", "dp", None),
        P("expert", "dp", None),
    )
    out_specs = P(("dp", "expert"), None)
    return jax.shard_map(body, mesh=mesh, in_specs=in_specs, out_specs=out_specs, check_vma=False)
```

```python
import functools

import jax
import jax.numpy as jnp
from jax import lax
from jax.experimental import pallas as pl
from jax.experimental.pallas import tpu as pltpu
from jax.sharding import PartitionSpec as P

EPSILON = 1e-05
EMPTY = 64.0
VMEM_LIMIT = 24 * 1024 * 1024
FIRST_SHARE = 9
LOCAL = pl.BlockSpec(memory_space=pltpu.VMEM)
FAR = pl.BlockSpec(memory_space=pltpu.HBM)
ANYWHERE = pl.BlockSpec(memory_space=pl.ANY)
BF16 = jnp.bfloat16
F32 = jnp.float32


def shape(*dims, dtype=BF16):
    return jax.ShapeDtypeStruct(dims, dtype)


def call(kernel, outs, args, flops, nbytes, in_specs=None, scratch=()):
    return pl.pallas_call(
        kernel,
        out_shape=tuple(outs),
        in_specs=[LOCAL] * len(args) if in_specs is None else in_specs,
        out_specs=(LOCAL,) * len(outs),
        scratch_shapes=list(scratch),
        compiler_params=pltpu.CompilerParams(vmem_limit_bytes=VMEM_LIMIT),
        cost_estimate=pl.CostEstimate(flops=flops, bytes_accessed=nbytes, transcendentals=0),
    )(*args)


def stay(array):
    return pltpu.with_memory_space_constraint(array, pltpu.HBM)


def fetch(sources, targets, sems):
    copies = [
        pltpu.make_async_copy(source, target, sems.at[i])
        for i, (source, target) in enumerate(zip(sources, targets))
    ]
    for copy in copies:
        copy.start()
    return copies


def earlier(count):
    i = lax.broadcasted_iota(jnp.int32, (count, count), 0)
    j = lax.broadcasted_iota(jnp.int32, (count, count), 1)
    return (i < j).astype(BF16)


def dot(a, b, dims=((1,), (0,))):
    return lax.dot_general(a, b, (dims, ((), ())), preferred_element_type=F32)


def put_slots(slots, refs, capacity):
    if len(refs) == 1:
        refs[0][...] = slots
        return
    for block in range(slots.shape[0] // capacity):
        row = block // 2 * capacity
        refs[block % 2][row : row + capacity] = slots[block * capacity : (block + 1) * capacity]


def get_blocks(refs):
    return jnp.concatenate([ref[...] for ref in refs], axis=0)


def pair_kernel(capacity, stay_ref, crossed_ref, _, *pair_refs):
    pairs = stay_ref.shape[0] // capacity
    for i in range(pairs):
        source = slice(i * capacity, (i + 1) * capacity)
        ref = pair_refs[i % len(pair_refs)]
        row = i // len(pair_refs) * 2 * capacity
        ref[row : row + capacity] = stay_ref[source]
        ref[row + capacity : row + 2 * capacity] = crossed_ref[source]


def pack_kernel(targets, experts, capacity, cut, *refs):
    assign_ref, tokens_ref, gain_ref = refs[:3]
    halves = refs[3 : 3 + targets], refs[3 + targets : 3 + 2 * targets]
    place_ref, gain_out, assign_buf, tokens_buf, sems = refs[3 + 2 * targets :]
    tok_count = tokens_ref.shape[0]
    slot_total = place_ref.shape[0]
    get_assign, *others = fetch(
        (assign_ref, tokens_ref, gain_ref),
        (assign_buf, tokens_buf, gain_out),
        sems,
    )
    get_assign.wait()
    assign = assign_buf[...]
    if targets == 2:
        assign = assign ^ lax.axis_index("expert")
    ids = lax.broadcasted_iota(jnp.int32, (experts, tok_count), 0)
    onehot = (assign == ids).astype(F32)
    before = dot(onehot.astype(BF16), earlier(tok_count))
    position = jnp.sum(before * onehot, axis=0, keepdims=True).astype(jnp.int32)
    rows = lax.broadcasted_iota(jnp.int32, (slot_total, tok_count), 0)
    place_ref[...] = (rows == assign_buf[...] * capacity + position).astype(F32).astype(BF16)
    place = (rows == assign * capacity + position).astype(F32)
    taken = jnp.sum(place, axis=1, keepdims=True)
    place = place.astype(BF16)
    for copy in others:
        copy.wait()
    packed = dot(place, tokens_buf[...])
    packed = jnp.where(taken > 0.5, packed, EMPTY).astype(BF16)
    put_slots(packed[:, :cut], halves[0], capacity)
    put_slots(packed[:, cut:], halves[1], capacity)


def load_kernel(inner_ref, outer_ref, _, inner_out, outer_out, sems):
    for copy in fetch((inner_ref, outer_ref), (inner_out, outer_out), sems):
        copy.wait()


def first_kernel(*refs):
    block_refs, (rows_ref, select_ref) = refs[:-2], refs[-2:]
    slots = get_blocks(block_refs)
    first = (lax.broadcasted_iota(jnp.int32, (8, 128), 1) == 0).astype(BF16)
    live = dot(first, slots[:, :128], ((1,), (1,))) < 0.5 * EMPTY
    rank = dot(live.astype(BF16), earlier(slots.shape[0]))
    rank = jnp.where(live, rank, -1.0)[:1].astype(jnp.int32)
    ids = lax.broadcasted_iota(jnp.int32, select_ref.shape, 0)
    select = (ids == rank).astype(BF16)
    select_ref[...] = select
    rows_ref[...] = dot(select, slots).astype(BF16)


def second_kernel(*refs):
    block_refs, (select_ref, rows_ref) = refs[:-2], refs[-2:]
    rows_ref[...] = dot(select_ref[...], get_blocks(block_refs)).astype(BF16)


def normalize(left, right, gain):
    count = left.shape[1] + right.shape[1]
    center = (
        jnp.sum(left, axis=1, keepdims=True) + jnp.sum(right, axis=1, keepdims=True)
    ) / count
    left, right = left - center, right - center
    spread = (
        jnp.sum(jnp.square(left), axis=1, keepdims=True)
        + jnp.sum(jnp.square(right), axis=1, keepdims=True)
    ) / count
    scale = lax.rsqrt(spread + EPSILON)
    cut = left.shape[1]
    left = (left * scale * gain[:, :cut]).astype(BF16)
    right = (right * scale * gain[:, cut:]).astype(BF16)
    return jnp.concatenate([left, right], axis=1)


def project(normed_ref, inner_ref, hidden_ref):
    units = inner_ref.shape[0]
    tile = min(units, 1024)
    for start in range(0, units, tile):
        act = dot(normed_ref[...], inner_ref[start : start + tile], ((1,), (1,)))
        hidden_ref[:, start : start + tile] = jnp.maximum(act, 0.0).astype(BF16)


def own_kernel(
    left_ref,
    right_ref,
    gain_ref,
    centroid_ref,
    inner_ref,
    outer_ref,
    left_out,
    right_out,
    gate_ref,
    normed_ref,
    hidden_ref,
):
    cut = left_ref.shape[1]
    left, right = left_ref[...].astype(F32), right_ref[...].astype(F32)
    centroid = centroid_ref[...].astype(F32)
    score = jnp.sum(left * centroid[:, :cut], axis=1, keepdims=True)
    score = score + jnp.sum(right * centroid[:, cut:], axis=1, keepdims=True)
    gate = (1.0 / (1.0 + jnp.exp(-score))).astype(BF16).astype(F32)
    gate_ref[...] = jnp.broadcast_to(gate, gate_ref.shape)
    normed_ref[...] = normalize(left, right, gain_ref[...])
    project(normed_ref, inner_ref, hidden_ref)
    cut = left_out.shape[1]
    left_out[...] = dot(hidden_ref[...], outer_ref[:, :cut]).astype(BF16)
    right_out[...] = dot(hidden_ref[...], outer_ref[:, cut:]).astype(BF16)


def guest_kernel(
    left_ref, right_ref, gain_ref, inner_ref, outer_ref, left_out, hidden_ref, normed_ref
):
    cut = left_out.shape[1]
    normed_ref[...] = normalize(
        left_ref[...].astype(F32), right_ref[...].astype(F32), gain_ref[...]
    )
    project(normed_ref, inner_ref, hidden_ref)
    left_out[...] = dot(hidden_ref[...], outer_ref[:, :cut]).astype(BF16)


def rest_kernel(hidden_ref, outer_ref, right_out):
    cut = outer_ref.shape[1] - right_out.shape[1]
    right_out[...] = dot(hidden_ref[...], outer_ref[:, cut:]).astype(BF16)


def spread_kernel(groups, capacity, relative, *refs):
    gate_ref, select_ref, slots_ref = refs[2 * groups :]
    sums = []
    for part_refs in (refs[:groups], refs[groups : 2 * groups]):
        total = part_refs[0][...].astype(F32)
        for ref in part_refs[1:]:
            total = total + ref[...].astype(F32)
        sums.append((gate_ref[:, :1] * total).astype(BF16))
    slots = dot(select_ref[...], jnp.concatenate(sums, axis=1), ((0,), (0,))).astype(BF16)
    if not relative:
        slots_ref[...] = slots
        return
    me = lax.axis_index("expert")
    for j in range(slots.shape[0] // capacity):
        row = pl.multiple_of((me ^ j) * capacity, capacity)
        slots_ref[pl.ds(row, capacity)] = slots[j * capacity : (j + 1) * capacity]


def final_kernel(tokens_ref, slots_ref, place_ref, out_ref):
    added = dot(place_ref[...], slots_ref[...], ((0,), (0,)))
    out_ref[...] = (tokens_ref[...].astype(F32) + added).astype(BF16)


def swap(array, axis_mask, experts):
    return lax.ppermute(array, "expert", [(i, i ^ axis_mask) for i in range(experts)])


def pair(stay, crossed, targets, capacity, after):
    rows, width = stay.shape
    return call(
        functools.partial(pair_kernel, capacity),
        [shape(2 * rows // targets, width) for _ in range(targets)],
        [stay, crossed, after],
        0,
        8 * rows * width,
        [LOCAL, LOCAL, ANYWHERE],
    )


def exchange(halves, experts, capacity, after=None):
    crossed = swap(halves[1], 1, experts)
    after = halves[0] if after is None else after
    blocks = list(pair(halves[0], crossed, experts // 2, capacity, after))
    for j in reversed(range(1, experts // 2)):
        blocks[j] = swap(blocks[j], 2 * j, experts)
    return blocks


def together(rows):
    return lax.all_to_all(rows, "expert", split_axis=0, concat_axis=0, tiled=True)


def body(tokens, assignment, centroids, norm_gain, inner_weight, outer_weight):
    tok_count, features = tokens.shape
    experts = lax.axis_size("expert")
    groups = lax.axis_size("dp")
    capacity = 2 * tok_count // experts
    slot_total = experts * capacity
    units = inner_weight.shape[1]
    targets = 2 if capacity % 16 == 0 and experts & (experts - 1) == 0 and experts >= 8 else 1
    cut = features // 128 * FIRST_SHARE // 16 * 128
    widths = (cut, features - cut)
    back_cut = (features // 128 * 3 + 3) // 4 * 128
    back_widths = (back_cut, features - back_cut)
    move_flops = slot_total * tok_count * features
    half_bytes = 2 * slot_total * features
    *packed, place, gain = call(
        functools.partial(pack_kernel, targets, experts, capacity, cut),
        [shape(slot_total // targets, w) for w in widths for _ in range(targets)]
        + [
            shape(slot_total, tok_count),
            pltpu.VMEM((1, features), F32),
        ],
        [stay(a) for a in (assignment.reshape(1, tok_count), tokens, norm_gain)],
        2 * move_flops,
        2 * half_bytes,
        [FAR] * 3,
        [
            pltpu.VMEM((1, tok_count), jnp.int32),
            pltpu.VMEM((tok_count, features), BF16),
            pltpu.SemaphoreType.DMA((3,)),
        ],
    )
    if targets == 2:
        first = exchange(packed[:targets], experts, capacity)
        second = exchange(packed[targets:], experts, capacity, first[experts // 4])
    else:
        first, second = [together(packed[0])], [together(packed[1])]
    rows, select = call(
        first_kernel,
        [shape(tok_count, cut), shape(tok_count, slot_total)],
        first,
        move_flops,
        half_bytes,
    )
    there = [[(i, (i + k) % groups) for i in range(groups)] for k in range(groups)]
    back = [[(t, s) for s, t in pairs] for pairs in there]
    left_guests = [lax.ppermute(rows, "dp", there[k]) for k in range(1, groups)]
    weights = (inner_weight[0], outer_weight[0])
    inner, outer = call(
        load_kernel,
        [pltpu.VMEM(w.shape, BF16) for w in weights],
        [stay(w) for w in weights] + [select],
        0,
        8 * units * features,
        [FAR, FAR, ANYWHERE],
        [pltpu.SemaphoreType.DMA((2,))],
    )
    (right_rows,) = call(
        second_kernel,
        [shape(tok_count, widths[1])],
        [*second, select],
        move_flops,
        half_bytes,
    )
    right_guests = [lax.ppermute(right_rows, "dp", there[k]) for k in range(1, groups)]
    ffn_flops = 4 * 2 * tok_count * units * features
    wide = [pltpu.VMEM((tok_count, features), BF16)]
    own_left, own_right, gate = call(
        own_kernel,
        [shape(tok_count, w) for w in back_widths] + [shape(tok_count, 128, dtype=F32)],
        [rows, right_rows, gain, centroids, inner, outer],
        ffn_flops,
        half_bytes,
        scratch=wide + [pltpu.VMEM((tok_count, units), BF16)],
    )
    left_parts, right_parts = [own_left], [own_right]
    for k in range(1, groups):
        left_part, hidden = call(
            guest_kernel,
            [shape(tok_count, back_cut), shape(tok_count, units)],
            [left_guests[k - 1], right_guests[k - 1], gain, inner, outer],
            ffn_flops * 3 // 4,
            half_bytes,
            scratch=wide,
        )
        left_parts.append(lax.ppermute(left_part, "dp", back[k]))
        (right_part,) = call(
            rest_kernel,
            [shape(tok_count, back_widths[1])],
            [hidden, outer],
            ffn_flops // 4,
            half_bytes,
        )
        right_parts.append(lax.ppermute(right_part, "dp", back[k]))
    (leaving,) = call(
        functools.partial(spread_kernel, groups, capacity, targets == 2),
        [shape(slot_total, features)],
        [*left_parts, *right_parts, gate, select],
        2 * move_flops,
        2 * half_bytes,
    )
    (out,) = call(
        final_kernel,
        [shape(tok_count, features)],
        [tokens, together(leaving), place],
        2 * move_flops,
        2 * half_bytes,
    )
    return out


def solution(mesh):
    in_specs = (
        P(("dp", "expert"), None),
        P(("dp", "expert")),
        P("expert", None),
        P("expert", None),
        P("expert", "dp", None),
        P("expert", "dp", None),
    )
    out_specs = P(("dp", "expert"), None)
    return jax.shard_map(body, mesh=mesh, in_specs=in_specs, out_specs=out_specs, check_vma=False)
```

```python
import functools

import jax
import jax.numpy as jnp
from jax import lax
from jax.experimental import pallas as pl
from jax.experimental.pallas import tpu as pltpu
from jax.sharding import PartitionSpec as P

EPSILON = 1e-05
EMPTY = 64.0
VMEM_LIMIT = 24 * 1024 * 1024
FIRST_SHARE = 9
LOCAL = pl.BlockSpec(memory_space=pltpu.VMEM)
FAR = pl.BlockSpec(memory_space=pltpu.HBM)
ANYWHERE = pl.BlockSpec(memory_space=pl.ANY)
BF16 = jnp.bfloat16
F32 = jnp.float32


def shape(*dims, dtype=BF16):
    return jax.ShapeDtypeStruct(dims, dtype)


def call(kernel, outs, args, flops, nbytes, in_specs=None, scratch=()):
    return pl.pallas_call(
        kernel,
        out_shape=tuple(outs),
        in_specs=[LOCAL] * len(args) if in_specs is None else in_specs,
        out_specs=(LOCAL,) * len(outs),
        scratch_shapes=list(scratch),
        compiler_params=pltpu.CompilerParams(vmem_limit_bytes=VMEM_LIMIT),
        cost_estimate=pl.CostEstimate(flops=flops, bytes_accessed=nbytes, transcendentals=0),
    )(*args)


def stay(array):
    return pltpu.with_memory_space_constraint(array, pltpu.HBM)


def fetch(sources, targets, sems):
    copies = [
        pltpu.make_async_copy(source, target, sems.at[i])
        for i, (source, target) in enumerate(zip(sources, targets))
    ]
    for copy in copies:
        copy.start()
    return copies


def earlier(count):
    i = lax.broadcasted_iota(jnp.int32, (count, count), 0)
    j = lax.broadcasted_iota(jnp.int32, (count, count), 1)
    return (i < j).astype(BF16)


def dot(a, b, dims=((1,), (0,))):
    return lax.dot_general(a, b, (dims, ((), ())), preferred_element_type=F32)


def put_slots(slots, refs, capacity):
    if len(refs) == 1:
        refs[0][...] = slots
        return
    for block in range(slots.shape[0] // capacity):
        row = block // 2 * capacity
        refs[block % 2][row : row + capacity] = slots[block * capacity : (block + 1) * capacity]


def get_blocks(refs):
    return jnp.concatenate([ref[...] for ref in refs], axis=0)


def pair_kernel(capacity, stay_ref, crossed_ref, _, *pair_refs):
    pairs = stay_ref.shape[0] // capacity
    for i in range(pairs):
        source = slice(i * capacity, (i + 1) * capacity)
        ref = pair_refs[i % len(pair_refs)]
        row = i // len(pair_refs) * 2 * capacity
        ref[row : row + capacity] = stay_ref[source]
        ref[row + capacity : row + 2 * capacity] = crossed_ref[source]


def pack_kernel(targets, experts, capacity, cut, *refs):
    assign_ref, tokens_ref, gain_ref = refs[:3]
    left_refs = refs[3 : 3 + targets]
    place_ref, packing_ref, gain_out, assign_buf, tokens_buf, sems = refs[3 + targets :]
    tok_count = tokens_ref.shape[0]
    slot_total = place_ref.shape[0]
    get_assign, *others = fetch(
        (assign_ref, tokens_ref.at[:, pl.ds(0, cut)], gain_ref),
        (assign_buf, tokens_buf, gain_out),
        sems,
    )
    get_assign.wait()
    assign = assign_buf[...]
    if targets == 2:
        assign = assign ^ lax.axis_index("expert")
    ids = lax.broadcasted_iota(jnp.int32, (experts, tok_count), 0)
    onehot = (assign == ids).astype(F32)
    before = dot(onehot.astype(BF16), earlier(tok_count))
    position = jnp.sum(before * onehot, axis=0, keepdims=True).astype(jnp.int32)
    rows = lax.broadcasted_iota(jnp.int32, (slot_total, tok_count), 0)
    place_ref[...] = (rows == assign_buf[...] * capacity + position).astype(F32).astype(BF16)
    place = (rows == assign * capacity + position).astype(F32)
    taken = jnp.sum(place, axis=1, keepdims=True)
    place = place.astype(BF16)
    packing_ref[...] = place
    for copy in others:
        copy.wait()
    packed = dot(place, tokens_buf[...])
    packed = jnp.where(taken > 0.5, packed, EMPTY).astype(BF16)
    put_slots(packed, left_refs, capacity)


def pack_rest_kernel(capacity, packing_ref, tokens_ref, *refs):
    *right_refs, tokens_buf, sems = refs
    width = tokens_buf.shape[1]
    cut = tokens_ref.shape[1] - width
    (copy,) = fetch((tokens_ref.at[:, pl.ds(cut, width)],), (tokens_buf,), sems)
    copy.wait()
    put_slots(dot(packing_ref[...], tokens_buf[...]).astype(BF16), right_refs, capacity)


def load_kernel(inner_ref, outer_ref, _, inner_out, outer_out, sems):
    for copy in fetch((inner_ref, outer_ref), (inner_out, outer_out), sems):
        copy.wait()


def first_kernel(*refs):
    block_refs, (rows_ref, select_ref) = refs[:-2], refs[-2:]
    slots = get_blocks(block_refs)
    first = (lax.broadcasted_iota(jnp.int32, (8, 128), 1) == 0).astype(BF16)
    live = dot(first, slots[:, :128], ((1,), (1,))) < 0.5 * EMPTY
    rank = dot(live.astype(BF16), earlier(slots.shape[0]))
    rank = jnp.where(live, rank, -1.0)[:1].astype(jnp.int32)
    ids = lax.broadcasted_iota(jnp.int32, select_ref.shape, 0)
    select = (ids == rank).astype(BF16)
    select_ref[...] = select
    rows_ref[...] = dot(select, slots).astype(BF16)


def second_kernel(*refs):
    block_refs, (select_ref, rows_ref) = refs[:-2], refs[-2:]
    rows_ref[...] = dot(select_ref[...], get_blocks(block_refs)).astype(BF16)


def normalize(left, right, gain):
    count = left.shape[1] + right.shape[1]
    center = (
        jnp.sum(left, axis=1, keepdims=True) + jnp.sum(right, axis=1, keepdims=True)
    ) / count
    left, right = left - center, right - center
    spread = (
        jnp.sum(jnp.square(left), axis=1, keepdims=True)
        + jnp.sum(jnp.square(right), axis=1, keepdims=True)
    ) / count
    scale = lax.rsqrt(spread + EPSILON)
    cut = left.shape[1]
    left = (left * scale * gain[:, :cut]).astype(BF16)
    right = (right * scale * gain[:, cut:]).astype(BF16)
    return jnp.concatenate([left, right], axis=1)


def project(normed_ref, inner_ref, hidden_ref):
    units = inner_ref.shape[0]
    tile = min(units, 1024)
    for start in range(0, units, tile):
        act = dot(normed_ref[...], inner_ref[start : start + tile], ((1,), (1,)))
        hidden_ref[:, start : start + tile] = jnp.maximum(act, 0.0).astype(BF16)


def own_kernel(
    left_ref,
    right_ref,
    gain_ref,
    centroid_ref,
    inner_ref,
    outer_ref,
    left_out,
    right_out,
    gate_ref,
    normed_ref,
    hidden_ref,
):
    cut = left_ref.shape[1]
    left, right = left_ref[...].astype(F32), right_ref[...].astype(F32)
    centroid = centroid_ref[...].astype(F32)
    score = jnp.sum(left * centroid[:, :cut], axis=1, keepdims=True)
    score = score + jnp.sum(right * centroid[:, cut:], axis=1, keepdims=True)
    gate = (1.0 / (1.0 + jnp.exp(-score))).astype(BF16).astype(F32)
    gate_ref[...] = jnp.broadcast_to(gate, gate_ref.shape)
    normed_ref[...] = normalize(left, right, gain_ref[...])
    project(normed_ref, inner_ref, hidden_ref)
    cut = left_out.shape[1]
    left_out[...] = dot(hidden_ref[...], outer_ref[:, :cut]).astype(BF16)
    right_out[...] = dot(hidden_ref[...], outer_ref[:, cut:]).astype(BF16)


def guest_kernel(
    left_ref, right_ref, gain_ref, inner_ref, outer_ref, left_out, hidden_ref, normed_ref
):
    cut = left_out.shape[1]
    normed_ref[...] = normalize(
        left_ref[...].astype(F32), right_ref[...].astype(F32), gain_ref[...]
    )
    project(normed_ref, inner_ref, hidden_ref)
    left_out[...] = dot(hidden_ref[...], outer_ref[:, :cut]).astype(BF16)


def rest_kernel(hidden_ref, outer_ref, right_out):
    cut = outer_ref.shape[1] - right_out.shape[1]
    right_out[...] = dot(hidden_ref[...], outer_ref[:, cut:]).astype(BF16)


def spread_kernel(groups, capacity, relative, *refs):
    gate_ref, select_ref, slots_ref = refs[2 * groups :]
    sums = []
    for part_refs in (refs[:groups], refs[groups : 2 * groups]):
        total = part_refs[0][...].astype(F32)
        for ref in part_refs[1:]:
            total = total + ref[...].astype(F32)
        sums.append((gate_ref[:, :1] * total).astype(BF16))
    slots = dot(select_ref[...], jnp.concatenate(sums, axis=1), ((0,), (0,))).astype(BF16)
    if not relative:
        slots_ref[...] = slots
        return
    me = lax.axis_index("expert")
    for j in range(slots.shape[0] // capacity):
        row = pl.multiple_of((me ^ j) * capacity, capacity)
        slots_ref[pl.ds(row, capacity)] = slots[j * capacity : (j + 1) * capacity]


def final_kernel(tokens_ref, slots_ref, place_ref, out_ref):
    added = dot(place_ref[...], slots_ref[...], ((0,), (0,)))
    out_ref[...] = (tokens_ref[...].astype(F32) + added).astype(BF16)


def swap(array, axis_mask, experts):
    return lax.ppermute(array, "expert", [(i, i ^ axis_mask) for i in range(experts)])


def pair(stay, crossed, targets, capacity, after):
    rows, width = stay.shape
    return call(
        functools.partial(pair_kernel, capacity),
        [shape(2 * rows // targets, width) for _ in range(targets)],
        [stay, crossed, after],
        0,
        8 * rows * width,
        [LOCAL, LOCAL, ANYWHERE],
    )


def exchange(halves, experts, capacity, after=None):
    crossed = swap(halves[1], 1, experts)
    after = halves[0] if after is None else after
    blocks = list(pair(halves[0], crossed, experts // 2, capacity, after))
    for j in reversed(range(1, experts // 2)):
        blocks[j] = swap(blocks[j], 2 * j, experts)
    return blocks


def together(rows):
    return lax.all_to_all(rows, "expert", split_axis=0, concat_axis=0, tiled=True)


def body(tokens, assignment, centroids, norm_gain, inner_weight, outer_weight):
    tok_count, features = tokens.shape
    experts = lax.axis_size("expert")
    groups = lax.axis_size("dp")
    capacity = 2 * tok_count // experts
    slot_total = experts * capacity
    units = inner_weight.shape[1]
    targets = 2 if capacity % 16 == 0 and experts & (experts - 1) == 0 and experts >= 8 else 1
    cut = features // 128 * FIRST_SHARE // 16 * 128
    widths = (cut, features - cut)
    back_cut = (features // 128 * 3 + 3) // 4 * 128
    back_widths = (back_cut, features - back_cut)
    move_flops = slot_total * tok_count * features
    half_bytes = 2 * slot_total * features
    *left_packed, place, packing, gain = call(
        functools.partial(pack_kernel, targets, experts, capacity, cut),
        [shape(slot_total // targets, cut) for _ in range(targets)]
        + [
            shape(slot_total, tok_count),
            shape(slot_total, tok_count),
            pltpu.VMEM((1, features), F32),
        ],
        [stay(a) for a in (assignment.reshape(1, tok_count), tokens, norm_gain)],
        2 * move_flops,
        2 * half_bytes,
        [FAR] * 3,
        [
            pltpu.VMEM((1, tok_count), jnp.int32),
            pltpu.VMEM((tok_count, cut), BF16),
            pltpu.SemaphoreType.DMA((3,)),
        ],
    )
    right_packed = call(
        functools.partial(pack_rest_kernel, capacity),
        [shape(slot_total // targets, widths[1]) for _ in range(targets)],
        [packing, stay(tokens)],
        move_flops,
        half_bytes,
        [LOCAL, FAR],
        [pltpu.VMEM((tok_count, widths[1]), BF16), pltpu.SemaphoreType.DMA((1,))],
    )
    if targets == 2:
        first = exchange(left_packed, experts, capacity)
        second = exchange(right_packed, experts, capacity, first[experts // 4])
    else:
        first, second = [together(left_packed[0])], [together(right_packed[0])]
    rows, select = call(
        first_kernel,
        [shape(tok_count, cut), shape(tok_count, slot_total)],
        first,
        move_flops,
        half_bytes,
    )
    there = [[(i, (i + k) % groups) for i in range(groups)] for k in range(groups)]
    back = [[(t, s) for s, t in pairs] for pairs in there]
    left_guests = [lax.ppermute(rows, "dp", there[k]) for k in range(1, groups)]
    weights = (inner_weight[0], outer_weight[0])
    inner, outer = call(
        load_kernel,
        [pltpu.VMEM(w.shape, BF16) for w in weights],
        [stay(w) for w in weights] + [select],
        0,
        8 * units * features,
        [FAR, FAR, ANYWHERE],
        [pltpu.SemaphoreType.DMA((2,))],
    )
    (right_rows,) = call(
        second_kernel,
        [shape(tok_count, widths[1])],
        [*second, select],
        move_flops,
        half_bytes,
    )
    right_guests = [lax.ppermute(right_rows, "dp", there[k]) for k in range(1, groups)]
    ffn_flops = 4 * 2 * tok_count * units * features
    wide = [pltpu.VMEM((tok_count, features), BF16)]
    own_left, own_right, gate = call(
        own_kernel,
        [shape(tok_count, w) for w in back_widths] + [shape(tok_count, 128, dtype=F32)],
        [rows, right_rows, gain, centroids, inner, outer],
        ffn_flops,
        half_bytes,
        scratch=wide + [pltpu.VMEM((tok_count, units), BF16)],
    )
    left_parts, right_parts = [own_left], [own_right]
    for k in range(1, groups):
        left_part, hidden = call(
            guest_kernel,
            [shape(tok_count, back_cut), shape(tok_count, units)],
            [left_guests[k - 1], right_guests[k - 1], gain, inner, outer],
            ffn_flops * 3 // 4,
            half_bytes,
            scratch=wide,
        )
        left_parts.append(lax.ppermute(left_part, "dp", back[k]))
        (right_part,) = call(
            rest_kernel,
            [shape(tok_count, back_widths[1])],
            [hidden, outer],
            ffn_flops // 4,
            half_bytes,
        )
        right_parts.append(lax.ppermute(right_part, "dp", back[k]))
    (leaving,) = call(
        functools.partial(spread_kernel, groups, capacity, targets == 2),
        [shape(slot_total, features)],
        [*left_parts, *right_parts, gate, select],
        2 * move_flops,
        2 * half_bytes,
    )
    (out,) = call(
        final_kernel,
        [shape(tok_count, features)],
        [tokens, together(leaving), place],
        2 * move_flops,
        2 * half_bytes,
    )
    return out


def solution(mesh):
    in_specs = (
        P(("dp", "expert"), None),
        P(("dp", "expert")),
        P("expert", None),
        P("expert", None),
        P("expert", "dp", None),
        P("expert", "dp", None),
    )
    out_specs = P(("dp", "expert"), None)
    return jax.shard_map(body, mesh=mesh, in_specs=in_specs, out_specs=out_specs, check_vma=False)
```
